128 devices in a mesh: row: 16 (over x_lo, z, core), col: 8 (over y, x_hi).
Axes of the slice: x: 4 (x_hi: 2, x_lo: 2; x = x_hi * 2 + x_lo), y: 4, z: 4, core: 2. Of those that a mesh axis runs over, the one named last changes fastest.
Arguments:
- features: bfloat16 [32768, 256], P(('col', 'row')), may hold values from -6 to 6
- weight: bfloat16 [256, 256], replicated, may hold values from -0.375 to 0.375
- bias: float32 [256], replicated, may hold values from -4 to 4
- tile_values: bfloat16 [16, 8, 384, 128, 128], P('row', 'col'), may hold values from -0.109375 to 0.109375
- tile_row: int32 [16, 8, 384], P('row', 'col'), may hold values from 0 to 15
- tile_col: int32 [16, 8, 384], P('row', 'col'), may hold values from 0 to 31
- tile_count: int32 [16, 8], P('row', 'col'), may hold values from 48 to 384, as said below
- cotangent: bfloat16 [32768, 256], P(('row', 'col')), may hold values from -6 to 6
Outputs:
- mixed: bfloat16 [32768, 256], P(('row', 'col'))
- weight_grad: float32 [256, 256], replicated
- bias_grad: float32 [256], replicated
- feature_grad: bfloat16 [32768, 256], P(('col', 'row'))
The draws below stay inside these ranges and needn't reach their ends.
Inputs may be any that keep to these rules, and one draw needn't show every extreme that they name: Only the first tile_count tiles of a device are used; some device uses all 384.
All inputs are finite; a program needn't handle non-finite values.
Results may differ from the reference program's by a relative error of at most 0.029.
Values may be sent and summed in bfloat16 or wider, within the bound.
No kernel may reach another device: no remote copies, remote signals or barrier semaphores. Data moves between devices by JAX's collectives and lax.ppermute only.
A program may use at most 128 MiB of HBM per device.

```python
import jax
import jax.numpy as jnp
from jax import lax

F = 256
TILE = 128
KT = 384
RB = 16
CB = 32
NODES = 32768
N_ROW = 16
N_COL = 8


def draw_tile_count(key, part):
    key = jax.random.fold_in(key, 7)
    first, second = jax.random.split(key)
    picks = jax.random.randint(first, (N_ROW, N_COL), 0, KT)
    counts = max(KT // 8, 1) + picks * picks // KT * 7 // 8
    chosen = jax.random.randint(second, (), 0, N_ROW * N_COL)
    flat = counts.reshape(-1)
    flat = jnp.where(jnp.arange(N_ROW * N_COL) == chosen, KT, flat)
    return flat.reshape(N_ROW, N_COL).astype(jnp.int32)


def place_ends(drawn, own_key, low, high):
    index_at = [jax.random.randint(jax.random.fold_in(own_key, axis), (), 0, length) for axis, length in enumerate(drawn.shape)]
    widest = drawn.shape.index(max(drawn.shape))
    next_to = index_at[:widest] + [(index_at[widest] + 1) % drawn.shape[widest]] + index_at[widest + 1:]
    return drawn.at[tuple(index_at)].set(low).at[tuple(next_to)].set(high)


def steps_of(key, shape, cuts, smallest, largest):
    level = 1.0
    for axis_at, blocks in cuts:
        draws = jax.random.uniform(jax.random.fold_in(jax.random.fold_in(key, 6), axis_at), (blocks,), jnp.float32, smallest / len(cuts), largest / len(cuts))
        level = level * jnp.repeat(jnp.exp(draws), shape[axis_at] // blocks).reshape((-1,) + (1,) * (len(shape) - 1 - axis_at))
    return level


def scatter_about(key, shape, spread, limit, cuts=(), held_as=jnp.bfloat16):
    array = spread * jax.random.normal(key, shape, jnp.float32)
    if cuts:
        array = array * steps_of(key, shape, cuts, -0.22, 0.18)
    return jnp.clip(array, -limit, limit).astype(held_as)


def setup_inputs(seed: int = 0) -> dict:
    key_list = jax.random.split(jax.random.key(seed), 9)
    return {
        "features": scatter_about(key_list[0], (NODES, F), 1.0, 6.0, ((0, 128),)),
        "weight": scatter_about(key_list[1], (F, F), F ** -0.5, 0.375),
        "bias": scatter_about(key_list[2], (F,), 1.0, 4.0, (), jnp.float32),
        "tile_values": scatter_about(key_list[3], (N_ROW, N_COL, KT, TILE, TILE), (TILE * KT // RB) ** -0.5, 0.109375, ((0, 16), (1, 8))),
        "tile_row": place_ends(jax.random.randint(key_list[4], (N_ROW, N_COL, KT), 0, RB), jax.random.fold_in(key_list[4], 1), 0, RB - 1).astype(jnp.int32),
        "tile_col": place_ends(jax.random.randint(key_list[5], (N_ROW, N_COL, KT), 0, CB), jax.random.fold_in(key_list[5], 1), 0, CB - 1).astype(jnp.int32),
        "tile_count": draw_tile_count(jax.random.fold_in(key_list[8], 71), 0),
        "cotangent": scatter_about(key_list[7], (NODES, F), 1.0, 6.0, ((0, 128),)),
    }


def apply_tiles(values, out_idx, in_idx, count, source, out_blocks, flipped):
    tile = values.shape[1]
    width = source.shape[1]
    blocks = source.reshape(-1, tile, width)
    total = values.shape[0]
    group = min(64, total)
    turns = total // group
    items = (values.reshape(turns, group, tile, tile), out_idx.reshape(turns, group), in_idx.reshape(turns, group), jnp.arange(total, dtype=jnp.int32).reshape(turns, group))
    form = 'kba,kbf->kaf' if flipped else 'kab,kbf->kaf'

    def step(acc, item):
        tiles, outs, ins, places = item
        picked = blocks[ins]
        prod = jnp.einsum(form, tiles.astype(jnp.float32), picked.astype(jnp.float32))
        live = (places < count).astype(jnp.float32)
        acc = acc.at[outs].add(prod * live[:, None, None])
        return (acc, None)
    acc = lax.scan(step, jnp.zeros((out_blocks, tile, width), jnp.float32), items)[0]
    return acc.reshape(out_blocks * tile, width)

def reference(features, weight, bias, tile_values, tile_row, tile_col, tile_count, cotangent):
    rows_len = RB * TILE
    cols_len = CB * TILE
    order = jnp.arange(N_ROW * N_COL, dtype=jnp.int32)

    def forward_step(acc, dev):
        i = dev // N_COL
        j = dev % N_COL
        panel = lax.dynamic_slice_in_dim(features, (j * cols_len).astype(jnp.int32), cols_len, 0)
        part = apply_tiles(tile_values[i, j], tile_row[i, j], tile_col[i, j], tile_count[i, j], panel, RB, False)
        part = lax.optimization_barrier(part.astype(jnp.bfloat16)).astype(jnp.float32)
        start = (i * rows_len).astype(jnp.int32)
        old = lax.dynamic_slice_in_dim(acc, start, rows_len, 0)
        return (lax.dynamic_update_slice_in_dim(acc, old + part, start, 0), None)
    summed = lax.scan(forward_step, jnp.zeros((NODES, F), jnp.float32), order)[0]
    aggregated = summed.astype(jnp.bfloat16)
    pre = jnp.dot(aggregated, weight, preferred_element_type=jnp.float32) + bias
    mixed = jax.nn.silu(pre).astype(jnp.bfloat16)
    sig = jax.nn.sigmoid(pre)
    slope = (cotangent.astype(jnp.float32) * sig * (1.0 + pre * (1.0 - sig))).astype(jnp.bfloat16)
    scale = 1.0 / jnp.sqrt(jnp.float32(NODES))
    weight_grad = jnp.dot(aggregated.T, slope, preferred_element_type=jnp.float32) * scale
    bias_grad = lax.optimization_barrier(jnp.sum(slope.astype(jnp.float32), axis=0)) * scale
    back = jnp.dot(slope, weight.T, preferred_element_type=jnp.float32).astype(jnp.bfloat16)

    def backward_step(acc, dev):
        i = dev // N_COL
        j = dev % N_COL
        rows = lax.dynamic_slice_in_dim(back, (i * rows_len).astype(jnp.int32), rows_len, 0)
        part = apply_tiles(tile_values[i, j], tile_col[i, j], tile_row[i, j], tile_count[i, j], rows, CB, True)
        part = lax.optimization_barrier(part.astype(jnp.bfloat16)).astype(jnp.float32)
        start = (j * cols_len).astype(jnp.int32)
        old = lax.dynamic_slice_in_dim(acc, start, cols_len, 0)
        return (lax.dynamic_update_slice_in_dim(acc, old + part, start, 0), None)
    grads = lax.scan(backward_step, jnp.zeros((NODES, F), jnp.float32), order)[0]
    return (mixed, weight_grad, bias_grad, grads.astype(jnp.bfloat16))
```

```python
import jax
import jax.numpy as jnp
from jax import lax
from jax.experimental import pallas as pl
from jax.experimental.pallas import tpu as pltpu
from jax.sharding import Mesh
from jax.sharding import PartitionSpec as P

TILE = 128
F = 256
KT = 384
RB = 16
CB = 32
SLOTS = 512
FWD = (4, 4)
BWD = (2, 8)
NODES = 32768

AXES = ("xl", "z", "k", "y", "xh")
SIZES = (2, 4, 2, 4, 2)
SHIFTS = (0, 1, 3, 2)

VM = pl.BlockSpec(memory_space=pltpu.VMEM)
SM = pl.BlockSpec(memory_space=pltpu.SMEM)


def shift(value, axis, by):
    n = SIZES[AXES.index(axis)]
    return lax.ppermute(value, axis, [(i, (i + by) % n) for i in range(n)])


def swap(value, axis, bit=1):
    n = SIZES[AXES.index(axis)]
    return lax.ppermute(value, axis, [(i, i ^ bit) for i in range(n)])


def order_one(key_col, key_row, other_col, chunk, spare):
    at = lambda shape, axis: lax.broadcasted_iota(jnp.int32, shape, axis)
    f32 = jnp.float32
    before = (key_col == key_row) & (at((KT, KT), 1) < at((KT, KT), 0))
    rank = jnp.sum(before.astype(f32), axis=1, keepdims=True)
    held = jnp.sum((key_row == at((128, KT), 0)).astype(f32), axis=1, keepdims=True)
    chunks = jnp.floor((held + (chunk - 1.0)) * (1.0 / chunk))
    lower = at((128, 128), 0) < at((128, 128), 1)
    starts = jnp.sum(jnp.where(lower, chunks, 0.0), axis=0, keepdims=True)
    mine = key_col == at((KT, 128), 1)
    start = jnp.sum(jnp.where(mine, starts, 0.0), axis=1, keepdims=True)
    place = (chunk * start + rank).astype(jnp.int32)
    live = key_col < 127
    hit = (place == at((KT, SLOTS), 1)) & live
    tiles = jnp.sum(jnp.where(hit, at((KT, SLOTS), 0).astype(f32), 0.0), axis=0, keepdims=True)
    less = jnp.where(hit, other_col.astype(f32) - spare, 0.0)
    others = jnp.sum(less, axis=0, keepdims=True) + spare
    opens = (place == chunk * at((KT, SLOTS), 1)) & live
    keys = jnp.sum(jnp.where(opens, key_col.astype(f32), 0.0), axis=0, keepdims=True)
    wide = jnp.concatenate([starts, jnp.zeros((1, SLOTS - 128), f32)], axis=1)
    return [tiles, others, keys, wide]


def order_kernel(count_ref, rc_ref, cc_ref, rr_ref, cr_ref, out_ref):
    count = count_ref[0, 0]
    live_c = lax.broadcasted_iota(jnp.int32, (KT, 1), 0) < count
    live_r = lax.broadcasted_iota(jnp.int32, (1, KT), 1) < count
    rc, cc, rr, cr = rc_ref[...], cc_ref[...], rr_ref[...], cr_ref[...]
    fwd = order_one(jnp.where(live_c, rc, 127), jnp.where(live_r, rr, 127), cc, FWD[0], CB)
    bwd = order_one(jnp.where(live_c, cc, 127), jnp.where(live_r, cr, 127), rc, BWD[0], RB)
    out_ref[...] = jnp.concatenate(fwd + bwd, axis=0).astype(jnp.int32)


def order(count, rows_idx, cols_idx):
    return pl.pallas_call(
        order_kernel,
        out_shape=jax.ShapeDtypeStruct((8, SLOTS), jnp.int32),
        in_specs=[SM, VM, VM, VM, VM],
        out_specs=VM,
        name="order_tiles",
    )(
        count,
        rows_idx.reshape(KT, 1),
        cols_idx.reshape(KT, 1),
        rows_idx.reshape(1, KT),
        cols_idx.reshape(1, KT),
    )


def forward_kernel(plan, here, own_ref, other_ref, values, out_ref, panel, acc):
    xl, z, k, y, xh = (here[n] for n in range(5))
    panel[CB] = jnp.zeros((TILE, F), jnp.bfloat16)
    for kk, ref in ((0, own_ref), (1, other_ref)):
        for s, by in enumerate(SHIFTS):
            for xx in range(2):
                piece = (
                    (jnp.bitwise_xor(xl, xx) * 4 + jnp.bitwise_and(z - by, 3)) * 2
                    + jnp.bitwise_xor(k, kk)
                )
                first = (s * 2 + xx) * 2 * TILE
                for h in range(2):
                    panel[2 * piece + h] = ref[first + h * TILE : first + (h + 1) * TILE, :]

    acc[...] = jnp.zeros_like(acc)
    chunk, group = FWD

    def step(q, _):
        found = []
        for u in range(group):
            base = (q * group + u) * chunk
            left = jnp.concatenate([values[plan[0, base + i]] for i in range(chunk)], axis=1)
            right = jnp.concatenate([panel[plan[1, base + i]] for i in range(chunk)], axis=0)
            found.append(jnp.dot(left, right, preferred_element_type=jnp.float32))
        for u in range(group):
            row = plan[2, q * group + u]
            acc[row] = acc[row] + found[u]
        return 0

    lax.fori_loop(0, lax.div(plan[3, RB] + (group - 1), group), step, 0)
    for n in range(RB):
        yy, xx, h = n // 4, (n // 2) % 2, n % 2
        row = (jnp.bitwise_and(y + yy, 3) * 2 + jnp.bitwise_xor(xh, xx)) * 2 + h
        out_ref[n] = acc[row].astype(jnp.bfloat16)


def forward(plan, here, own, other, values):
    return pl.pallas_call(
        forward_kernel,
        out_shape=jax.ShapeDtypeStruct((RB, TILE, F), jnp.bfloat16),
        in_specs=[SM, SM, VM, VM, VM],
        out_specs=VM,
        scratch_shapes=[
            pltpu.VMEM((CB + 1, TILE, F), jnp.bfloat16),
            pltpu.VMEM((RB, TILE, F), jnp.float32),
        ],
        compiler_params=pltpu.CompilerParams(vmem_limit_bytes=40 << 20),
        name="forward_tiles",
    )(plan, here, own, other, values)


def dense_kernel(near, far, weight, bias, cot, mixed_ref, back_ref, grads_ref):
    f32 = jnp.float32
    agg = (near[...] + far[...].astype(f32)).astype(jnp.bfloat16)
    w = weight[...]
    pre = jnp.dot(agg, w, preferred_element_type=f32) + bias[...]
    sig = jax.nn.sigmoid(pre)
    mixed_ref[...] = (pre * sig).astype(jnp.bfloat16)
    slope = (cot[...].astype(f32) * sig * (1.0 + pre * (1.0 - sig))).astype(jnp.bfloat16)
    back = lax.dot_general(slope, w, (((1,), (1,)), ((), ())), preferred_element_type=f32)
    back_ref[...] = back.astype(jnp.bfloat16)
    wsum = lax.dot_general(agg, slope, (((0,), (0,)), ((), ())), preferred_element_type=f32)
    bsum = jnp.sum(slope.astype(f32), axis=0, keepdims=True)
    grads_ref[0:F, :] = wsum.astype(jnp.bfloat16)
    grads_ref[F : F + 16, :] = jnp.broadcast_to(bsum, (16, F)).astype(jnp.bfloat16)


def dense(near, far, weight, bias, cot):
    return pl.pallas_call(
        dense_kernel,
        out_shape=(
            jax.ShapeDtypeStruct((F, F), jnp.bfloat16),
            jax.ShapeDtypeStruct((F, F), jnp.bfloat16),
            jax.ShapeDtypeStruct((F + 16, F), jnp.bfloat16),
        ),
        in_specs=[VM] * 5,
        out_specs=(VM, VM, VM),
        name="dense_part",
    )(near, far, weight, bias.reshape(1, F), cot)


def backward_kernel(plan, here, ref, values, own_ref, other_ref, panel, acc):
    xl, z, k, y, xh = (here[n] for n in range(5))
    panel[RB] = jnp.zeros((TILE, F), jnp.bfloat16)
    for s, by in enumerate(SHIFTS):
        for xx in range(2):
            piece = jnp.bitwise_and(y - by, 3) * 2 + jnp.bitwise_xor(xh, xx)
            first = (s * 2 + xx) * 2 * TILE
            for h in range(2):
                panel[2 * piece + h] = ref[first + h * TILE : first + (h + 1) * TILE, :]
    acc[...] = jnp.zeros_like(acc)
    chunk, group = BWD

    def step(q, _):
        found = []
        for u in range(group):
            base = (q * group + u) * chunk
            left = jnp.concatenate([values[plan[4, base + i]] for i in range(chunk)], axis=0)
            right = jnp.concatenate([panel[plan[5, base + i]] for i in range(chunk)], axis=0)
            found.append(
                lax.dot_general(
                    left, right, (((0,), (0,)), ((), ())), preferred_element_type=jnp.float32
                )
            )
        for u in range(group):
            col = plan[6, q * group + u]
            acc[col] = acc[col] + found[u]
        return 0

    lax.fori_loop(0, lax.div(plan[7, CB] + (group - 1), group), step, 0)
    for kk, out_ref in ((1, other_ref), (0, own_ref)):
        for n in range(CB // 2):
            zz, xx, h = n // 4, (n // 2) % 2, n % 2
            col = (
                (jnp.bitwise_xor(xl, xx) * 4 + jnp.bitwise_and(z + zz, 3)) * 2
                + jnp.bitwise_xor(k, kk)
            ) * 2 + h
            out_ref[n] = acc[col].astype(jnp.bfloat16)


def backward(plan, here, pieces, values):
    half = jax.ShapeDtypeStruct((CB // 2, TILE, F), jnp.bfloat16)
    return pl.pallas_call(
        backward_kernel,
        out_shape=(half, half),
        in_specs=[SM, SM, VM, VM],
        out_specs=(VM, VM),
        scratch_shapes=[
            pltpu.VMEM((RB + 1, TILE, F), jnp.bfloat16),
            pltpu.VMEM((CB, TILE, F), jnp.float32),
        ],
        compiler_params=pltpu.CompilerParams(vmem_limit_bytes=40 << 20),
        name="backward_tiles",
    )(plan, here, pieces, values)


def gather(piece, pair_axis, ring_axis):
    both = jnp.concatenate([piece, swap(piece, pair_axis)], axis=0)
    parts = [both] + [shift(both, ring_axis, by) for by in SHIFTS[1:]]
    return jnp.concatenate(parts, axis=0)


def scatter_sum(parts, pair_axis, ring_axis):
    f32 = jnp.float32
    half = parts[0].shape[0] // 2
    got = [shift(parts[by], ring_axis, by) for by in (1, 2, 3)]
    total = parts[0].astype(f32) + got[0].astype(f32) + got[1].astype(f32) + got[2].astype(f32)
    far = swap(total[half:].astype(jnp.bfloat16), pair_axis)
    return total[:half], far


def all_sum(value):
    for axis, bit in (("k", 1), ("xl", 1), ("z", 1), ("z", 2), ("xh", 1), ("y", 1), ("y", 2)):
        got = swap(value, axis, bit)
        value = (value.astype(jnp.float32) + got.astype(jnp.float32)).astype(jnp.bfloat16)
    return value


def on_device(features, weight, bias, tile_values, tile_row, tile_col, tile_count, cotangent):
    f32 = jnp.float32
    values = tile_values[0, 0]
    here = jnp.stack([lax.axis_index(a) for a in AXES] + [jnp.int32(0)] * 3).astype(jnp.int32)
    plan = order(tile_count, tile_row[0, 0], tile_col[0, 0])

    own = gather(features, "xl", "z")
    other = swap(own, "k")
    partial = forward(plan, here, own, other, values).reshape(4, 2 * F, F)
    near, far = scatter_sum([partial[n] for n in range(4)], "xh", "y")
    mixed, back, grads = dense(near, far, weight, bias, cotangent)

    pieces = gather(back, "xh", "y")
    part_own, part_other = backward(plan, here, pieces, values)
    got = swap(part_other, "k")
    both = (part_own.astype(f32) + got.astype(f32)).astype(jnp.bfloat16)
    both = both.reshape(4, 2 * F, F)
    near, far = scatter_sum([both[n] for n in range(4)], "xl", "z")
    feature_grad = (near + far.astype(f32)).astype(jnp.bfloat16)

    grads = all_sum(grads)
    scale = 1.0 / jnp.sqrt(f32(NODES))
    grads = grads.astype(f32) * scale
    return (mixed, grads[:F], grads[F], feature_grad)


def solution(mesh):
    fine = Mesh(mesh.devices.reshape(SIZES), AXES)
    row, col = ("xl", "z", "k"), ("y", "xh")
    in_specs = (
        P(col + row, None),
        P(),
        P(),
        P(row, col, None, None, None),
        P(row, col, None),
        P(row, col, None),
        P(row, col),
        P(row + col, None),
    )
    out_specs = (P(row + col, None), P(), P(), P(col + row, None))
    return jax.shard_map(
        on_device, mesh=fine, in_specs=in_specs, out_specs=out_specs, check_vma=False
    )
```

```python
import functools

import jax
import jax.numpy as jnp
from jax import lax
from jax.experimental import pallas as pl
from jax.experimental.pallas import tpu as pltpu
from jax.sharding import Mesh
from jax.sharding import PartitionSpec as P

TILE = 128
F = 256
KT = 384
RB = 16
CB = 32
SLOTS = 512
FWD = (4, 4)
BWD = (2, 8)
NODES = 32768

AXES = ("xl", "z", "k", "y", "xh")
SIZES = (2, 4, 2, 4, 2)
SHIFTS = (0, 1, 3, 2)

VM = pl.BlockSpec(memory_space=pltpu.VMEM)
SM = pl.BlockSpec(memory_space=pltpu.SMEM)


def shift(value, axis, by):
    n = SIZES[AXES.index(axis)]
    return lax.ppermute(value, axis, [(i, (i + by) % n) for i in range(n)])


def swap(value, axis, bit=1):
    n = SIZES[AXES.index(axis)]
    return lax.ppermute(value, axis, [(i, i ^ bit) for i in range(n)])


def order_one(key_col, key_row, other_col, chunk, spare):
    at = lambda shape, axis: lax.broadcasted_iota(jnp.int32, shape, axis)
    f32 = jnp.float32
    before = (key_col == key_row) & (at((KT, KT), 1) < at((KT, KT), 0))
    rank = jnp.sum(before.astype(f32), axis=1, keepdims=True)
    held = jnp.sum((key_row == at((128, KT), 0)).astype(f32), axis=1, keepdims=True)
    chunks = jnp.floor((held + (chunk - 1.0)) * (1.0 / chunk))
    lower = at((128, 128), 0) < at((128, 128), 1)
    starts = jnp.sum(jnp.where(lower, chunks, 0.0), axis=0, keepdims=True)
    mine = key_col == at((KT, 128), 1)
    start = jnp.sum(jnp.where(mine, starts, 0.0), axis=1, keepdims=True)
    place = (chunk * start + rank).astype(jnp.int32)
    live = key_col < 127
    hit = (place == at((KT, SLOTS), 1)) & live
    tiles = jnp.sum(jnp.where(hit, at((KT, SLOTS), 0).astype(f32), 0.0), axis=0, keepdims=True)
    less = jnp.where(hit, other_col.astype(f32) - spare, 0.0)
    others = jnp.sum(less, axis=0, keepdims=True) + spare
    opens = (place == chunk * at((KT, SLOTS), 1)) & live
    keys = jnp.sum(jnp.where(opens, key_col.astype(f32), 0.0), axis=0, keepdims=True)
    wide = jnp.concatenate([starts, jnp.zeros((1, SLOTS - 128), f32)], axis=1)
    return [tiles, others, keys, wide]


def row_key(row, here):
    piece = row >> 1
    yy = jnp.bitwise_and((piece >> 1) - here[3], 3)
    xx = jnp.bitwise_xor(jnp.bitwise_and(piece, 1), here[4])
    turn = jnp.where(yy == 2, 0, jnp.where(yy == 0, 3, (yy + 1) >> 1))
    return turn * 4 + xx * 2 + jnp.bitwise_and(row, 1)


def col_key(col, here):
    piece = col >> 1
    kk = jnp.bitwise_xor(jnp.bitwise_and(piece, 1), here[2])
    zz = jnp.bitwise_and((piece >> 1) - here[1], 3)
    far = jnp.where(zz == 2, 0, jnp.where(zz == 0, 3, (zz + 1) >> 1))
    turn = jnp.where(kk == 1, far, 4 + jnp.bitwise_and(far + 1, 3))
    xx = jnp.bitwise_xor(piece >> 3, here[0])
    return turn * 4 + xx * 2 + jnp.bitwise_and(col, 1)


def order_kernel(count_ref, here, rr_ref, cr_ref, values, fwd_ref, bwd_ref, held, sem):
    copy = pltpu.make_async_copy(values, held, sem)
    copy.start()
    count = count_ref[0, 0]
    live_c = lax.broadcasted_iota(jnp.int32, (KT, 1), 0) < count
    live_r = lax.broadcasted_iota(jnp.int32, (1, KT), 1) < count
    rr, cr = rr_ref[...], cr_ref[...]
    both = jnp.concatenate([rr, cr] * 4, axis=0).astype(jnp.float32).T.astype(jnp.int32)
    rc, cc = both[:, 0:1], both[:, 1:2]
    key = lambda of, idx, live: jnp.where(live, of(idx, here), 127)
    fwd = order_one(key(row_key, rc, live_c), key(row_key, rr, live_r), cc, FWD[0], CB)
    bwd = order_one(key(col_key, cc, live_c), key(col_key, cr, live_r), rc, BWD[0], RB)
    fwd_ref[...] = jnp.concatenate(fwd, axis=0).astype(jnp.int32)
    bwd_ref[...] = jnp.concatenate(bwd, axis=0).astype(jnp.int32)
    copy.wait()


def order(count, here, rows_idx, cols_idx, values):
    table = jax.ShapeDtypeStruct((4, SLOTS), jnp.int32)
    return pl.pallas_call(
        order_kernel,
        out_shape=(table, table, pltpu.VMEM((KT, TILE, TILE), jnp.bfloat16)),
        in_specs=[SM, SM, VM, VM, pl.BlockSpec(memory_space=pltpu.HBM)],
        out_specs=(VM, VM, VM),
        scratch_shapes=[pltpu.SemaphoreType.DMA],
        compiler_params=pltpu.CompilerParams(vmem_limit_bytes=8 << 20),
        name="order_tiles",
    )(
        count,
        here,
        rows_idx.reshape(1, KT),
        cols_idx.reshape(1, KT),
        pltpu.with_memory_space_constraint(values, pltpu.HBM),
    )


def products(flip, first, plan, panel, values, outs, extra, acc):
    chunk, group = BWD if flip else FWD
    keys = sum(out.shape[0] for out in outs) // TILE
    acc[...] = jnp.zeros_like(acc)
    low, high = plan[3, first], plan[3, first + keys]

    def step(q, _):
        found = []
        for u in range(group):
            base = (low + q * group + u) * chunk
            tiles = [values[plan[0, base + i]] for i in range(chunk)]
            right = jnp.concatenate([panel[plan[1, base + i]] for i in range(chunk)], axis=0)
            if flip:
                left, dims = jnp.concatenate(tiles, axis=0), (((0,), (0,)), ((), ()))
            else:
                left, dims = jnp.concatenate(tiles, axis=1), (((1,), (0,)), ((), ()))
            found.append(lax.dot_general(left, right, dims, preferred_element_type=jnp.float32))
        for u in range(group):
            at = low + q * group + u
            target = jnp.where(at < high, plan[2, at] - first, keys)
            acc[target] = acc[target] + found[u]
        return 0

    lax.fori_loop(0, lax.div(high - low + (group - 1), group), step, 0)
    n = 0
    for out in outs:
        for r in range(0, out.shape[0], TILE):
            block = acc[n]
            if extra is not None:
                ref, base = extra
                block = block.astype(jnp.bfloat16).astype(jnp.float32)
                block += ref[base + n * TILE : base + (n + 1) * TILE, :].astype(jnp.float32)
            out[r : r + TILE, :] = block.astype(out.dtype)
            n += 1


def forward_first(first, plan, here, own_ref, other_ref, values, out_ref, panel, acc):
    xl, z, k = (here[n] for n in range(3))
    panel[CB] = jnp.zeros((TILE, F), jnp.bfloat16)
    for kk, ref in ((0, own_ref), (1, other_ref)):
        for s, by in enumerate(SHIFTS):
            for xx in range(2):
                piece = (
                    (jnp.bitwise_xor(xl, xx) * 4 + jnp.bitwise_and(z - by, 3)) * 2
                    + jnp.bitwise_xor(k, kk)
                )
                base = (s * 2 + xx) * 2 * TILE
                for h in range(2):
                    panel[2 * piece + h] = ref[base + h * TILE : base + (h + 1) * TILE, :]
    products(False, first, plan, panel, values, (out_ref,), None, acc)


def backward_first(first, plan, here, ref, values, out_ref, panel, acc):
    y, xh = here[3], here[4]
    panel[RB] = jnp.zeros((TILE, F), jnp.bfloat16)
    for s, by in enumerate(SHIFTS):
        for xx in range(2):
            piece = jnp.bitwise_and(y - by, 3) * 2 + jnp.bitwise_xor(xh, xx)
            base = (s * 2 + xx) * 2 * TILE
            for h in range(2):
                panel[2 * piece + h] = ref[base + h * TILE : base + (h + 1) * TILE, :]
    products(True, first, plan, panel, values, (out_ref,), None, acc)


def later(flip, first, n_outs, base, plan, panel, values, *refs):
    extra = None if base is None else (refs[0], base)
    outs = refs[-1 - n_outs : -1]
    products(flip, first, plan, panel, values, outs, extra, refs[-1])


COST = pl.CostEstimate(flops=1000, bytes_accessed=1000, transcendentals=0)
PARAMS = pltpu.CompilerParams(vmem_limit_bytes=16 << 20)


def rows_of(*blocks, dtype=jnp.bfloat16):
    return tuple(jax.ShapeDtypeStruct((n * TILE, F), dtype) for n in blocks)


def call_first(kernel, name, first, keys, blocks, plan, here, pieces, values):
    return pl.pallas_call(
        functools.partial(kernel, first),
        out_shape=rows_of(keys) + (pltpu.VMEM((blocks + 1, TILE, F), jnp.bfloat16),),
        in_specs=[SM, SM] + [VM] * len(pieces) + [VM],
        out_specs=(VM, VM),
        scratch_shapes=[pltpu.VMEM((keys + 1, TILE, F), jnp.float32)],
        compiler_params=PARAMS,
        cost_estimate=COST,
        name=name,
    )(plan, here, *pieces, values)


def call_later(flip, name, first, outs, plan, panel, values, add=None, base=None, after=()):
    keys = sum(o.shape[0] for o in outs) // TILE
    adds = () if add is None else (add,)
    return pl.pallas_call(
        functools.partial(later, flip, first, len(outs), base),
        out_shape=outs,
        in_specs=[SM, VM, VM] + [VM] * len(adds) + [pl.BlockSpec(memory_space=pl.ANY)] * len(after),
        out_specs=(VM,) * len(outs),
        scratch_shapes=[pltpu.VMEM((keys + 1, TILE, F), jnp.float32)],
        compiler_params=PARAMS,
        cost_estimate=COST,
        name=name,
    )(plan, panel, values, *adds, *after)


def dense_kernel(near, far, weight, bias, cot, mixed_ref, back_ref, grads_ref):
    f32 = jnp.float32
    agg = (near[...] + far[...].astype(f32)).astype(jnp.bfloat16)
    w = weight[...]
    pre = jnp.dot(agg, w, preferred_element_type=f32) + bias[...]
    sig = jax.nn.sigmoid(pre)
    mixed_ref[...] = (pre * sig).astype(jnp.bfloat16)
    slope = (cot[...].astype(f32) * sig * (1.0 + pre * (1.0 - sig))).astype(jnp.bfloat16)
    back = lax.dot_general(slope, w, (((1,), (1,)), ((), ())), preferred_element_type=f32)
    back_ref[...] = back.astype(jnp.bfloat16)
    wsum = lax.dot_general(agg, slope, (((0,), (0,)), ((), ())), preferred_element_type=f32)
    bsum = jnp.sum(slope.astype(f32), axis=0, keepdims=True)
    grads_ref[0:F, :] = wsum.astype(jnp.bfloat16)
    grads_ref[F : F + 16, :] = jnp.broadcast_to(bsum, (16, F)).astype(jnp.bfloat16)


def dense(near, far, weight, bias, cot):
    return pl.pallas_call(
        dense_kernel,
        out_shape=(
            jax.ShapeDtypeStruct((F, F), jnp.bfloat16),
            jax.ShapeDtypeStruct((F, F), jnp.bfloat16),
            jax.ShapeDtypeStruct((F + 16, F), jnp.bfloat16),
        ),
        in_specs=[VM] * 5,
        out_specs=(VM, VM, VM),
        compiler_params=pltpu.CompilerParams(vmem_limit_bytes=8 << 20),
        name="dense_part",
    )(near, far, weight, bias.reshape(1, F), cot)


def gather(piece, pair_axis, ring_axis):
    both = jnp.concatenate([piece, swap(piece, pair_axis)], axis=0)
    parts = [both] + [shift(both, ring_axis, by) for by in SHIFTS[1:]]
    return jnp.concatenate(parts, axis=0)


def tie(value, *others):
    return lax.optimization_barrier((value,) + others)[0]


def add_up(value, axis, bit=1, after=()):
    got = tie(swap(value, axis, bit), *after)
    return (value.astype(jnp.float32) + got.astype(jnp.float32)).astype(jnp.bfloat16)


def on_device(features, weight, bias, tile_values, tile_row, tile_col, tile_count, cotangent):
    f32, bf16 = jnp.float32, jnp.bfloat16
    here = jnp.stack([lax.axis_index(a) for a in AXES] + [jnp.int32(0)] * 3).astype(jnp.int32)
    plan, turned, values = order(
        tile_count, here, tile_row[0, 0], tile_col[0, 0], tile_values[0, 0]
    )

    own = gather(features, "xl", "z")
    own = tie(own, plan, turned)
    other = swap(own, "k")
    part, panel = call_first(forward_first, "rows_y2", 0, 4, CB, plan, here, (own, other), values)
    got = shift(part, "y", 2)
    one, three = call_later(False, "rows_y1_y3", 4, rows_of(4, 4), plan, panel, values)
    one, three = shift(one, "y", 1), shift(three, "y", 3)
    (total,) = call_later(
        False, "rows_y0", 12, rows_of(4, dtype=f32), plan, panel, values, add=got, base=0
    )
    total = total + one.astype(f32) + three.astype(f32)
    far = swap(total[F:].astype(bf16), "xh")
    mixed, back, grads = dense(total[:F], far, weight, bias, cotangent)

    pieces = gather(back, "xh", "y")
    for axis, bit in (("k", 1), ("xl", 1), ("z", 1)):
        grads = add_up(grads, axis, bit)
    sent, panel = call_first(
        backward_first, "columns_far", 0, 12, RB, turned, here, (pieces,), values
    )
    grads = add_up(grads, "z", 2, (sent,))
    got = swap(sent, "k")
    sent, zero = call_later(True, "columns_z0", 12, rows_of(4, 4), turned, panel, values)
    grads = add_up(grads, "xh", 1, (zero,))
    total = zero.astype(f32) + swap(sent, "k").astype(f32)
    (two,) = call_later(True, "columns_z2", 20, rows_of(4), turned, panel, values, got, 0)
    two = shift(two, "z", 2)
    one, three = call_later(
        True, "columns_z1_z3", 24, rows_of(4, 4), turned, panel, values, got, 4 * TILE
    )
    grads = add_up(grads, "y", 1, (one,))
    one, three = shift(one, "z", 1), shift(three, "z", 3)
    total = total + two.astype(f32) + one.astype(f32) + three.astype(f32)
    far = swap(total[F:].astype(bf16), "xl")
    feature_grad = (total[:F] + far.astype(f32)).astype(bf16)

    grads = add_up(grads, "y", 2)
    scale = 1.0 / jnp.sqrt(f32(NODES))
    grads = grads.astype(f32) * scale
    return (mixed, grads[:F], grads[F], feature_grad)


def solution(mesh):
    fine = Mesh(mesh.devices.reshape(SIZES), AXES)
    row, col = ("xl", "z", "k"), ("y", "xh")
    in_specs = (
        P(col + row, None),
        P(),
        P(),
        P(row, col, None, None, None),
        P(row, col, None),
        P(row, col, None),
        P(row, col),
        P(row + col, None),
    )
    out_specs = (P(row + col, None), P(), P(), P(col + row, None))
    return jax.shard_map(
        on_device, mesh=fine, in_specs=in_specs, out_specs=out_specs, check_vma=False
    )
```

```python
import functools

import jax
import jax.numpy as jnp
from jax import lax
from jax.experimental import pallas as pl
from jax.experimental.pallas import tpu as pltpu
from jax.sharding import Mesh
from jax.sharding import PartitionSpec as P

TILE = 128
F = 256
KT = 384
RB = 16
CB = 32
SLOTS = 512
FWD = (4, 8)
BWD = (2, 16)
NODES = 32768

AXES = ("xl", "z", "k", "y", "xh")
SIZES = (2, 4, 2, 4, 2)
SHIFTS = (0, 2, 1, 3)

VM = pl.BlockSpec(memory_space=pltpu.VMEM)
SM = pl.BlockSpec(memory_space=pltpu.SMEM)


def shift(value, axis, by):
    n = SIZES[AXES.index(axis)]
    return lax.ppermute(value, axis, [(i, (i + by) % n) for i in range(n)])


def swap(value, axis, bit=1):
    n = SIZES[AXES.index(axis)]
    return lax.ppermute(value, axis, [(i, i ^ bit) for i in range(n)])


def order_one(key_col, key_row, other_col, chunk, spare):
    at = lambda shape, axis: lax.broadcasted_iota(jnp.int32, shape, axis)
    f32 = jnp.float32
    before = (key_col == key_row) & (at((KT, KT), 1) < at((KT, KT), 0))
    rank = jnp.sum(before.astype(f32), axis=1, keepdims=True)
    held = jnp.sum((key_row == at((128, KT), 0)).astype(f32), axis=1, keepdims=True)
    chunks = jnp.floor((held + (chunk - 1.0)) * (1.0 / chunk))
    lower = at((128, 128), 0) < at((128, 128), 1)
    starts = jnp.sum(jnp.where(lower, chunks, 0.0), axis=0, keepdims=True)
    mine = key_col == at((KT, 128), 1)
    start = jnp.sum(jnp.where(mine, starts, 0.0), axis=1, keepdims=True)
    place = (chunk * start + rank).astype(jnp.int32)
    live = key_col < 127
    hit = (place == at((KT, SLOTS), 1)) & live
    tiles = jnp.sum(jnp.where(hit, at((KT, SLOTS), 0).astype(f32), 0.0), axis=0, keepdims=True)
    less = jnp.where(hit, other_col.astype(f32) - spare, 0.0)
    others = jnp.sum(less, axis=0, keepdims=True) + spare
    opens = (place == chunk * at((KT, SLOTS), 1)) & live
    keys = jnp.sum(jnp.where(opens, key_col.astype(f32), 0.0), axis=0, keepdims=True)
    wide = jnp.concatenate([starts, jnp.zeros((1, SLOTS - 128), f32)], axis=1)
    return [tiles, others, keys, wide]


def row_key(row, here):
    piece = row >> 1
    yy = jnp.bitwise_and((piece >> 1) - here[3], 3)
    xx = jnp.bitwise_xor(jnp.bitwise_and(piece, 1), here[4])
    turn = jnp.where(yy == 2, 0, jnp.where(yy == 0, 3, (yy + 1) >> 1))
    return turn * 4 + xx * 2 + jnp.bitwise_and(row, 1)


def col_key(col, here):
    piece = col >> 1
    kk = jnp.bitwise_xor(jnp.bitwise_and(piece, 1), here[2])
    zz = jnp.bitwise_and((piece >> 1) - here[1], 3)
    far = jnp.where(zz == 2, 0, jnp.where(zz == 0, 3, (zz + 1) >> 1))
    turn = jnp.where(kk == 1, far, 4 + jnp.bitwise_and(far + 1, 3))
    xx = jnp.bitwise_xor(piece >> 3, here[0])
    return turn * 4 + xx * 2 + jnp.bitwise_and(col, 1)


def order_kernel(count_ref, here, rr_ref, cr_ref, values, fwd_ref, bwd_ref, held, sem):
    copy = pltpu.make_async_copy(values, held, sem)
    copy.start()
    count = count_ref[0, 0]
    live_c = lax.broadcasted_iota(jnp.int32, (KT, 1), 0) < count
    live_r = lax.broadcasted_iota(jnp.int32, (1, KT), 1) < count
    rr, cr = rr_ref[...], cr_ref[...]
    both = jnp.concatenate([rr, cr] * 4, axis=0).astype(jnp.float32).T.astype(jnp.int32)
    rc, cc = both[:, 0:1], both[:, 1:2]
    key = lambda of, idx, live: jnp.where(live, of(idx, here), 127)
    fwd = order_one(key(row_key, rc, live_c), key(row_key, rr, live_r), cc, FWD[0], CB)
    bwd = order_one(key(col_key, cc, live_c), key(col_key, cr, live_r), rc, BWD[0], RB)
    fwd_ref[...] = jnp.concatenate(fwd, axis=0).astype(jnp.int32)
    bwd_ref[...] = jnp.concatenate(bwd, axis=0).astype(jnp.int32)
    copy.wait()


def order(count, here, rows_idx, cols_idx, values):
    table = jax.ShapeDtypeStruct((4, SLOTS), jnp.int32)
    return pl.pallas_call(
        order_kernel,
        out_shape=(table, table, pltpu.VMEM((KT, TILE, TILE), jnp.bfloat16)),
        in_specs=[SM, SM, VM, VM, pl.BlockSpec(memory_space=pltpu.HBM)],
        out_specs=(VM, VM, VM),
        scratch_shapes=[pltpu.SemaphoreType.DMA],
        compiler_params=pltpu.CompilerParams(vmem_limit_bytes=8 << 20),
        name="order_tiles",
    )(
        count,
        here,
        pltpu.with_memory_space_constraint(rows_idx.reshape(1, KT), pltpu.HBM),
        pltpu.with_memory_space_constraint(cols_idx.reshape(1, KT), pltpu.HBM),
        pltpu.with_memory_space_constraint(values, pltpu.HBM),
    )


def products(flip, first, plan, panel, values, outs, extra, acc):
    chunk, group = BWD if flip else FWD
    keys = sum(out.shape[0] for out in outs) // TILE
    acc[...] = jnp.zeros_like(acc)
    low, high = plan[3, first], plan[3, first + keys]

    def step(q, _):
        found = []
        for u in range(group):
            base = (low + q * group + u) * chunk
            tiles = [values[plan[0, base + i]] for i in range(chunk)]
            right = jnp.concatenate([panel[plan[1, base + i]] for i in range(chunk)], axis=0)
            if flip:
                left, dims = jnp.concatenate(tiles, axis=0), (((0,), (0,)), ((), ()))
            else:
                left, dims = jnp.concatenate(tiles, axis=1), (((1,), (0,)), ((), ()))
            found.append(lax.dot_general(left, right, dims, preferred_element_type=jnp.float32))
        for u in range(group):
            at = low + q * group + u
            target = jnp.where(at < high, plan[2, at] - first, keys)
            acc[target] = acc[target] + found[u]
        return 0

    lax.fori_loop(0, lax.div(high - low + (group - 1), group), step, 0)
    n = 0
    for out in outs:
        for r in range(0, out.shape[0], TILE):
            block = acc[n]
            if extra is not None:
                ref, base = extra
                block = block.astype(jnp.bfloat16).astype(jnp.float32)
                block += ref[base + n * TILE : base + (n + 1) * TILE, :].astype(jnp.float32)
            out[r : r + TILE, :] = block.astype(out.dtype)
            n += 1


def forward_first(first, plan, here, own_ref, other_ref, values, out_ref, panel, acc):
    xl, z, k = (here[n] for n in range(3))
    panel[CB] = jnp.zeros((TILE, F), jnp.bfloat16)
    for kk, ref in ((0, own_ref), (1, other_ref)):
        for s, by in enumerate(SHIFTS):
            for xx in range(2):
                piece = (
                    (jnp.bitwise_xor(xl, xx) * 4 + jnp.bitwise_and(z - by, 3)) * 2
                    + jnp.bitwise_xor(k, kk)
                )
                base = (s * 2 + xx) * 2 * TILE
                for h in range(2):
                    panel[2 * piece + h] = ref[base + h * TILE : base + (h + 1) * TILE, :]
    products(False, first, plan, panel, values, (out_ref,), None, acc)


def backward_first(first, plan, here, ref, values, out_ref, panel, acc):
    y, xh = here[3], here[4]
    panel[RB] = jnp.zeros((TILE, F), jnp.bfloat16)
    for s, by in enumerate(SHIFTS):
        for xx in range(2):
            piece = jnp.bitwise_and(y - by, 3) * 2 + jnp.bitwise_xor(xh, xx)
            base = (s * 2 + xx) * 2 * TILE
            for h in range(2):
                panel[2 * piece + h] = ref[base + h * TILE : base + (h + 1) * TILE, :]
    products(True, first, plan, panel, values, (out_ref,), None, acc)


def later(flip, first, n_outs, base, plan, panel, values, *refs):
    extra = None if base is None else (refs[0], base)
    outs = refs[-1 - n_outs : -1]
    products(flip, first, plan, panel, values, outs, extra, refs[-1])


def cost(keys, targets):
    flops = keys * 2 * KT * TILE * TILE * F // targets
    return pl.CostEstimate(flops=4 * flops, bytes_accessed=1000, transcendentals=0)


PARAMS = pltpu.CompilerParams(vmem_limit_bytes=16 << 20)


def rows_of(*blocks, dtype=jnp.bfloat16):
    return tuple(jax.ShapeDtypeStruct((n * TILE, F), dtype) for n in blocks)


def call_first(kernel, name, first, keys, blocks, plan, here, pieces, values):
    return pl.pallas_call(
        functools.partial(kernel, first),
        out_shape=rows_of(keys) + (pltpu.VMEM((blocks + 1, TILE, F), jnp.bfloat16),),
        in_specs=[SM, SM] + [VM] * len(pieces) + [VM],
        out_specs=(VM, VM),
        scratch_shapes=[pltpu.VMEM((keys + 1, TILE, F), jnp.float32)],
        compiler_params=PARAMS,
        cost_estimate=cost(keys, 48 - blocks),
        name=name,
    )(plan, here, *pieces, values)


def call_later(flip, name, first, outs, plan, panel, values, add=None, base=None, after=()):
    keys = sum(o.shape[0] for o in outs) // TILE
    adds = () if add is None else (add,)
    return pl.pallas_call(
        functools.partial(later, flip, first, len(outs), base),
        out_shape=outs,
        in_specs=[SM, VM, VM] + [VM] * len(adds) + [pl.BlockSpec(memory_space=pl.ANY)] * len(after),
        out_specs=(VM,) * len(outs),
        scratch_shapes=[pltpu.VMEM((keys + 1, TILE, F), jnp.float32)],
        compiler_params=PARAMS,
        cost_estimate=cost(keys, CB if flip else RB),
        name=name,
    )(plan, panel, values, *adds, *after)


def dense_kernel(near, far, weight, bias, cot, mixed_ref, back_ref, grads_ref):
    f32 = jnp.float32
    agg = (near[...] + far[...].astype(f32)).astype(jnp.bfloat16)
    w = weight[...]
    pre = jnp.dot(agg, w, preferred_element_type=f32) + bias[...]
    sig = jax.nn.sigmoid(pre)
    mixed_ref[...] = (pre * sig).astype(jnp.bfloat16)
    slope = (cot[...].astype(f32) * sig * (1.0 + pre * (1.0 - sig))).astype(jnp.bfloat16)
    back = lax.dot_general(slope, w, (((1,), (1,)), ((), ())), preferred_element_type=f32)
    back_ref[...] = back.astype(jnp.bfloat16)
    wsum = lax.dot_general(agg, slope, (((0,), (0,)), ((), ())), preferred_element_type=f32)
    bsum = jnp.sum(slope.astype(f32), axis=0, keepdims=True)
    grads_ref[0:F, :] = wsum.astype(jnp.bfloat16)
    grads_ref[F : F + 16, :] = jnp.broadcast_to(bsum, (16, F)).astype(jnp.bfloat16)


def dense(near, far, weight, bias, cot):
    return pl.pallas_call(
        dense_kernel,
        out_shape=(
            jax.ShapeDtypeStruct((F, F), jnp.bfloat16),
            jax.ShapeDtypeStruct((F, F), jnp.bfloat16),
            jax.ShapeDtypeStruct((F + 16, F), jnp.bfloat16),
        ),
        in_specs=[VM] * 5,
        out_specs=(VM, VM, VM),
        compiler_params=pltpu.CompilerParams(vmem_limit_bytes=8 << 20),
        name="dense_part",
    )(near, far, weight, bias.reshape(1, F), cot)


def gather(piece, pair_axis, ring_axis):
    both = jnp.concatenate([piece, swap(piece, pair_axis)], axis=0)
    parts = [both] + [shift(both, ring_axis, by) for by in SHIFTS[1:]]
    return jnp.concatenate(parts, axis=0)


def tie(value, *others):
    return lax.optimization_barrier((value,) + others)[0]


def add_up(value, axis, bit=1, after=()):
    got = tie(swap(value, axis, bit), *after)
    return (value.astype(jnp.float32) + got.astype(jnp.float32)).astype(jnp.bfloat16)


def on_device(features, weight, bias, tile_values, tile_row, tile_col, tile_count, cotangent):
    f32, bf16 = jnp.float32, jnp.bfloat16
    here = jnp.stack([lax.axis_index(a) for a in AXES] + [jnp.int32(0)] * 3).astype(jnp.int32)
    plan, turned, values = order(
        tile_count, here, tile_row[0, 0], tile_col[0, 0], tile_values[0, 0]
    )

    own = gather(features, "xl", "z")
    own = tie(own, plan, turned)
    other = swap(own, "k")
    part, panel = call_first(forward_first, "rows_y2", 0, 4, CB, plan, here, (own, other), values)
    got = shift(part, "y", 2)
    one, three = call_later(False, "rows_y1_y3", 4, rows_of(4, 4), plan, panel, values)
    one, three = shift(one, "y", 1), shift(three, "y", 3)
    (total,) = call_later(
        False, "rows_y0", 12, rows_of(4, dtype=f32), plan, panel, values, add=got, base=0
    )
    total = total + one.astype(f32) + three.astype(f32)
    far = swap(total[F:].astype(bf16), "xh")
    mixed, back, grads = dense(total[:F], far, weight, bias, cotangent)

    pieces = gather(back, "xh", "y")
    for axis, bit in (("k", 1), ("z", 2), ("z", 1)):
        grads = add_up(grads, axis, bit)
    sent, panel = call_first(
        backward_first, "columns_far", 0, 12, RB, turned, here, (pieces,), values
    )
    grads = add_up(grads, "xl", 1, (sent,))
    got = swap(sent, "k")
    sent, zero = call_later(True, "columns_z0", 12, rows_of(4, 4), turned, panel, values)
    total = zero.astype(f32) + swap(sent, "k").astype(f32)
    (two,) = call_later(True, "columns_z2", 20, rows_of(4), turned, panel, values, got, 0)
    two = shift(two, "z", 2)
    one, three = call_later(
        True, "columns_z1_z3", 24, rows_of(4, 4), turned, panel, values, got, 4 * TILE
    )
    grads = add_up(grads, "xh", 1, (one,))
    one, three = shift(one, "z", 1), shift(three, "z", 3)
    total = total + two.astype(f32) + one.astype(f32) + three.astype(f32)
    far = swap(total[F:].astype(bf16), "xl")
    feature_grad = (total[:F] + far.astype(f32)).astype(bf16)

    grads = add_up(add_up(grads, "y", 1), "y", 2)
    scale = 1.0 / jnp.sqrt(f32(NODES))
    grads = grads.astype(f32) * scale
    return (mixed, grads[:F], grads[F], feature_grad)


def solution(mesh):
    fine = Mesh(mesh.devices.reshape(SIZES), AXES)
    row, col = ("xl", "z", "k"), ("y", "xh")
    in_specs = (
        P(col + row, None),
        P(),
        P(),
        P(row, col, None, None, None),
        P(row, col, None),
        P(row, col, None),
        P(row, col),
        P(row + col, None),
    )
    out_specs = (P(row + col, None), P(), P(), P(col + row, None))
    return jax.shard_map(
        on_device, mesh=fine, in_specs=in_specs, out_specs=out_specs, check_vma=False
    )
```

```python
import functools

import jax
import jax.numpy as jnp
from jax import lax
from jax.experimental import pallas as pl
from jax.experimental.pallas import tpu as pltpu
from jax.sharding import Mesh
from jax.sharding import PartitionSpec as P

TILE = 128
F = 256
KT = 384
RB = 16
CB = 32
SLOTS = 512
FWD = (4, 8)
BWD = (2, 16)
NODES = 32768

AXES = ("xl", "z", "k", "y", "xh")
SIZES = (2, 4, 2, 4, 2)
SHIFTS = (0, 2, 1, 3)

VM = pl.BlockSpec(memory_space=pltpu.VMEM)
SM = pl.BlockSpec(memory_space=pltpu.SMEM)


def shift(value, axis, by):
    n = SIZES[AXES.index(axis)]
    return lax.ppermute(value, axis, [(i, (i + by) % n) for i in range(n)])


def swap(value, axis, bit=1):
    n = SIZES[AXES.index(axis)]
    return lax.ppermute(value, axis, [(i, i ^ bit) for i in range(n)])


def order_one(key_col, key_row, other_col, chunk, spare):
    at = lambda shape, axis: lax.broadcasted_iota(jnp.int32, shape, axis)
    f32 = jnp.float32
    before = (key_col == key_row) & (at((KT, KT), 1) < at((KT, KT), 0))
    rank = jnp.sum(before.astype(f32), axis=1, keepdims=True)
    held = jnp.sum((key_row == at((128, KT), 0)).astype(f32), axis=1, keepdims=True)
    chunks = jnp.floor((held + (chunk - 1.0)) * (1.0 / chunk))
    lower = at((128, 128), 0) < at((128, 128), 1)
    starts = jnp.sum(jnp.where(lower, chunks, 0.0), axis=0, keepdims=True)
    mine = key_col == at((KT, 128), 1)
    start = jnp.sum(jnp.where(mine, starts, 0.0), axis=1, keepdims=True)
    place = (chunk * start + rank).astype(jnp.int32)
    live = key_col < 127
    hit = (place == at((KT, SLOTS), 1)) & live
    tiles = jnp.sum(jnp.where(hit, at((KT, SLOTS), 0).astype(f32), 0.0), axis=0, keepdims=True)
    less = jnp.where(hit, other_col.astype(f32) - spare, 0.0)
    others = jnp.sum(less, axis=0, keepdims=True) + spare
    opens = (place == chunk * at((KT, SLOTS), 1)) & live
    keys = jnp.sum(jnp.where(opens, key_col.astype(f32), 0.0), axis=0, keepdims=True)
    wide = jnp.concatenate([starts, jnp.zeros((1, SLOTS - 128), f32)], axis=1)
    return [tiles, others, keys, wide]


def row_key(row, here):
    piece = row >> 1
    yy = jnp.bitwise_and((piece >> 1) - here[3], 3)
    xx = jnp.bitwise_xor(jnp.bitwise_and(piece, 1), here[4])
    turn = jnp.where(yy == 2, 0, jnp.where(yy == 0, 3, (yy + 1) >> 1))
    return turn * 4 + xx * 2 + jnp.bitwise_and(row, 1)


def col_key(col, here):
    piece = col >> 1
    kk = jnp.bitwise_xor(jnp.bitwise_and(piece, 1), here[2])
    zz = jnp.bitwise_and((piece >> 1) - here[1], 3)
    far = jnp.where(zz == 2, 0, jnp.where(zz == 0, 3, (zz + 1) >> 1))
    turn = jnp.where(kk == 1, far, 4 + jnp.bitwise_and(far + 1, 3))
    xx = jnp.bitwise_xor(piece >> 3, here[0])
    return turn * 4 + xx * 2 + jnp.bitwise_and(col, 1)


def order_kernel(count_ref, here, rr_ref, cr_ref, values, fwd_ref, bwd_ref, held, sem):
    copy = pltpu.make_async_copy(values, held, sem)
    copy.start()
    count = count_ref[0, 0]
    live_c = lax.broadcasted_iota(jnp.int32, (KT, 1), 0) < count
    live_r = lax.broadcasted_iota(jnp.int32, (1, KT), 1) < count
    rr, cr = rr_ref[...], cr_ref[...]
    both = jnp.concatenate([rr, cr] * 4, axis=0).astype(jnp.float32).T.astype(jnp.int32)
    rc, cc = both[:, 0:1], both[:, 1:2]
    key = lambda of, idx, live: jnp.where(live, of(idx, here), 127)
    fwd = order_one(key(row_key, rc, live_c), key(row_key, rr, live_r), cc, FWD[0], CB)
    bwd = order_one(key(col_key, cc, live_c), key(col_key, cr, live_r), rc, BWD[0], RB)
    fwd_ref[...] = jnp.concatenate(fwd, axis=0).astype(jnp.int32)
    bwd_ref[...] = jnp.concatenate(bwd, axis=0).astype(jnp.int32)
    copy.wait()


def order(count, here, rows_idx, cols_idx, values):
    table = jax.ShapeDtypeStruct((4, SLOTS), jnp.int32)
    return pl.pallas_call(
        order_kernel,
        out_shape=(table, table, pltpu.VMEM((KT, TILE, TILE), jnp.bfloat16)),
        in_specs=[SM, SM, VM, VM, pl.BlockSpec(memory_space=pltpu.HBM)],
        out_specs=(VM, VM, VM),
        scratch_shapes=[pltpu.SemaphoreType.DMA],
        compiler_params=pltpu.CompilerParams(vmem_limit_bytes=8 << 20),
        name="order_tiles",
    )(
        count,
        here,
        pltpu.with_memory_space_constraint(rows_idx.reshape(1, KT), pltpu.HBM),
        pltpu.with_memory_space_constraint(cols_idx.reshape(1, KT), pltpu.HBM),
        pltpu.with_memory_space_constraint(values, pltpu.HBM),
    )


def products(flip, first, plan, panel, values, outs, extra, acc):
    chunk, group = BWD if flip else FWD
    keys = sum(out.shape[0] for out in outs) // TILE
    acc[...] = jnp.zeros_like(acc)
    low, high = plan[3, first], plan[3, first + keys]

    def step(q, _):
        found = []
        for u in range(group):
            base = (low + q * group + u) * chunk
            tiles = [values[plan[0, base + i]] for i in range(chunk)]
            right = jnp.concatenate([panel[plan[1, base + i]] for i in range(chunk)], axis=0)
            if flip:
                left, dims = jnp.concatenate(tiles, axis=0), (((0,), (0,)), ((), ()))
            else:
                left, dims = jnp.concatenate(tiles, axis=1), (((1,), (0,)), ((), ()))
            found.append(lax.dot_general(left, right, dims, preferred_element_type=jnp.float32))
        for u in range(group):
            at = low + q * group + u
            target = jnp.where(at < high, plan[2, at] - first, keys)
            acc[target] = acc[target] + found[u]
        return 0

    lax.fori_loop(0, lax.div(high - low + (group - 1), group), step, 0)
    n = 0
    for out in outs:
        for r in range(0, out.shape[0], TILE):
            block = acc[n]
            if extra is not None:
                ref, base = extra
                block = block.astype(jnp.bfloat16).astype(jnp.float32)
                block += ref[base + n * TILE : base + (n + 1) * TILE, :].astype(jnp.float32)
            out[r : r + TILE, :] = block.astype(out.dtype)
            n += 1


def forward_first(first, plan, here, own_ref, other_ref, values, out_ref, panel, acc):
    xl, z, k = (here[n] for n in range(3))
    panel[CB] = jnp.zeros((TILE, F), jnp.bfloat16)
    for kk, ref in ((0, own_ref), (1, other_ref)):
        for s, by in enumerate(SHIFTS):
            for xx in range(2):
                piece = (
                    (jnp.bitwise_xor(xl, xx) * 4 + jnp.bitwise_and(z - by, 3)) * 2
                    + jnp.bitwise_xor(k, kk)
                )
                base = (s * 2 + xx) * 2 * TILE
                for h in range(2):
                    panel[2 * piece + h] = ref[base + h * TILE : base + (h + 1) * TILE, :]
    products(False, first, plan, panel, values, (out_ref,), None, acc)


def backward_first(first, plan, here, ref, values, out_ref, panel, acc):
    y, xh = here[3], here[4]
    panel[RB] = jnp.zeros((TILE, F), jnp.bfloat16)
    for s, by in enumerate(SHIFTS):
        for xx in range(2):
            piece = jnp.bitwise_and(y - by, 3) * 2 + jnp.bitwise_xor(xh, xx)
            base = (s * 2 + xx) * 2 * TILE
            for h in range(2):
                panel[2 * piece + h] = ref[base + h * TILE : base + (h + 1) * TILE, :]
    products(True, first, plan, panel, values, (out_ref,), None, acc)


def later(flip, first, n_outs, base, plan, panel, values, *refs):
    extra = None if base is None else (refs[0], base)
    outs = refs[-1 - n_outs : -1]
    products(flip, first, plan, panel, values, outs, extra, refs[-1])


def cost(keys, targets):
    flops = keys * 2 * KT * TILE * TILE * F // targets
    return pl.CostEstimate(flops=4 * flops, bytes_accessed=1000, transcendentals=0)


PARAMS = pltpu.CompilerParams(vmem_limit_bytes=16 << 20)


def rows_of(*blocks, dtype=jnp.bfloat16):
    return tuple(jax.ShapeDtypeStruct((n * TILE, F), dtype) for n in blocks)


def call_first(kernel, name, first, keys, blocks, plan, here, pieces, values):
    return pl.pallas_call(
        functools.partial(kernel, first),
        out_shape=rows_of(keys) + (pltpu.VMEM((blocks + 1, TILE, F), jnp.bfloat16),),
        in_specs=[SM, SM] + [VM] * len(pieces) + [VM],
        out_specs=(VM, VM),
        scratch_shapes=[pltpu.VMEM((keys + 1, TILE, F), jnp.float32)],
        compiler_params=PARAMS,
        cost_estimate=cost(keys, 48 - blocks),
        name=name,
    )(plan, here, *pieces, values)


def call_later(flip, name, first, outs, plan, panel, values, add=None, base=None, after=()):
    keys = sum(o.shape[0] for o in outs) // TILE
    adds = () if add is None else (add,)
    return pl.pallas_call(
        functools.partial(later, flip, first, len(outs), base),
        out_shape=outs,
        in_specs=[SM, VM, VM] + [VM] * len(adds) + [pl.BlockSpec(memory_space=pl.ANY)] * len(after),
        out_specs=(VM,) * len(outs),
        scratch_shapes=[pltpu.VMEM((keys + 1, TILE, F), jnp.float32)],
        compiler_params=PARAMS,
        cost_estimate=cost(keys, CB if flip else RB),
        name=name,
    )(plan, panel, values, *adds, *after)


def dense_kernel(mine, theirs, weight, bias, cot, far_cot, mixed_ref, back_ref, grads_ref):
    f32, bf16 = jnp.float32, jnp.bfloat16
    turned = jnp.concatenate([theirs[F : 2 * F, :], theirs[0:F, :]], axis=0)
    agg = (mine[...].astype(f32) + turned.astype(f32)).astype(bf16)
    w = weight[...]
    pre = jnp.dot(agg, w, preferred_element_type=f32) + bias[...]
    sig = jax.nn.sigmoid(pre)
    mixed_ref[...] = (pre[:F] * sig[:F]).astype(bf16)
    both_cot = jnp.concatenate([cot[...], far_cot[...]], axis=0).astype(f32)
    slope = (both_cot * sig * (1.0 + pre * (1.0 - sig))).astype(bf16)
    back = lax.dot_general(slope, w, (((1,), (1,)), ((), ())), preferred_element_type=f32)
    back_ref[...] = back.astype(bf16)
    wsum = lax.dot_general(
        agg[:F], slope[:F], (((0,), (0,)), ((), ())), preferred_element_type=f32
    )
    bsum = jnp.sum(slope[:F].astype(f32), axis=0, keepdims=True)
    grads_ref[0:F, :] = wsum.astype(bf16)
    grads_ref[F : F + 16, :] = jnp.broadcast_to(bsum, (16, F)).astype(bf16)


def dense(mine, theirs, weight, bias, cot, far_cot):
    return pl.pallas_call(
        dense_kernel,
        out_shape=(
            jax.ShapeDtypeStruct((F, F), jnp.bfloat16),
            jax.ShapeDtypeStruct((2 * F, F), jnp.bfloat16),
            jax.ShapeDtypeStruct((F + 16, F), jnp.bfloat16),
        ),
        in_specs=[VM] * 6,
        out_specs=(VM, VM, VM),
        compiler_params=pltpu.CompilerParams(vmem_limit_bytes=8 << 20),
        name="dense_part",
    )(mine, theirs, weight, bias.reshape(1, F), cot, far_cot)


def gather(both, ring_axis):
    parts = [both] + [shift(both, ring_axis, by) for by in SHIFTS[1:]]
    return jnp.concatenate(parts, axis=0)


def tie(value, *others):
    return lax.optimization_barrier((value,) + others)[0]


def add_up(value, axis, bit=1, after=()):
    got = tie(swap(value, axis, bit), *after)
    return (value.astype(jnp.float32) + got.astype(jnp.float32)).astype(jnp.bfloat16)


def on_device(features, weight, bias, tile_values, tile_row, tile_col, tile_count, cotangent):
    f32, bf16 = jnp.float32, jnp.bfloat16
    here = jnp.stack([lax.axis_index(a) for a in AXES] + [jnp.int32(0)] * 3).astype(jnp.int32)
    plan, turned, values = order(
        tile_count, here, tile_row[0, 0], tile_col[0, 0], tile_values[0, 0]
    )

    own = gather(jnp.concatenate([features, swap(features, "xl")], axis=0), "z")
    far_cot = swap(cotangent, "xh")
    own = tie(own, plan, turned, far_cot)
    other = swap(own, "k")
    part, panel = call_first(forward_first, "rows_y2", 0, 4, CB, plan, here, (own, other), values)
    got = shift(part, "y", 2)
    one, three = call_later(False, "rows_y1_y3", 4, rows_of(4, 4), plan, panel, values)
    one, three = shift(one, "y", 1), shift(three, "y", 3)
    (total,) = call_later(
        False, "rows_y0", 12, rows_of(4, dtype=f32), plan, panel, values, add=got, base=0
    )
    total = total + one.astype(f32) + three.astype(f32)
    total = total.astype(bf16)
    mixed, back, grads = dense(total, swap(total, "xh"), weight, bias, cotangent, far_cot)

    pieces = gather(back, "y")
    for axis, bit in (("k", 1), ("z", 2),):
        grads = add_up(grads, axis, bit)
    sent, panel = call_first(
        backward_first, "columns_far", 0, 12, RB, turned, here, (pieces,), values
    )
    grads = add_up(grads, "z", 1, (sent,))
    got = swap(sent, "k")
    sent, zero = call_later(True, "columns_z0", 12, rows_of(4, 4), turned, panel, values)
    total = zero.astype(f32) + swap(sent, "k").astype(f32)
    (two,) = call_later(True, "columns_z2", 20, rows_of(4), turned, panel, values, got, 0)
    two = shift(two, "z", 2)
    one, three = call_later(
        True, "columns_z1_z3", 24, rows_of(4, 4), turned, panel, values, got, 4 * TILE
    )
    grads = add_up(grads, "xl", 1, (one,))
    one, three = shift(one, "z", 1), shift(three, "z", 3)
    total = total + two.astype(f32) + one.astype(f32) + three.astype(f32)
    far = swap(total[F:].astype(bf16), "xl")
    feature_grad = (total[:F] + far.astype(f32)).astype(bf16)

    grads = add_up(add_up(grads, "xh"), "y", 2)
    got = swap(grads, "y", 1)
    scale = 1.0 / jnp.sqrt(f32(NODES))
    weight_grad = (grads[:F].astype(f32) + got[:F].astype(f32)) * scale
    bias_grad = (grads[F].astype(f32) + got[F].astype(f32)) * scale
    return (mixed, weight_grad, bias_grad, feature_grad)


def solution(mesh):
    fine = Mesh(mesh.devices.reshape(SIZES), AXES)
    row, col = ("xl", "z", "k"), ("y", "xh")
    in_specs = (
        P(col + row, None),
        P(),
        P(),
        P(row, col, None, None, None),
        P(row, col, None),
        P(row, col, None),
        P(row, col),
        P(row + col, None),
    )
    out_specs = (P(row + col, None), P(), P(), P(col + row, None))
    return jax.shard_map(
        on_device, mesh=fine, in_specs=in_specs, out_specs=out_specs, check_vma=False
    )
```
